32 devices in a mesh: ctx: 8 (over y, x, core), exp: 4 (over z).
Axes of the slice: x: 2, y: 2, z: 4, core: 2. Of those that a mesh axis runs over, the one named last changes fastest.
Arguments:
- latent: bfloat16 [1024, 576], P('ctx'), may hold values from -8 to 8
- query: bfloat16 [1024, 12288], P('ctx', 'exp'), may hold values from -8 to 8
- w_uk: bfloat16 [64, 512, 128], P('exp'), may hold values from -0.5 to 0.5
- w_uv: bfloat16 [64, 512, 128], P('exp'), may hold values from -0.25 to 0.25
- w_o: bfloat16 [8192, 4096], P('exp'), may hold values from -0.0625 to 0.0625
- residual: bfloat16 [1024, 4096], P('ctx', 'exp'), may hold values from -16 to 16
- norm_gain: float32 [4096], P('exp'), may hold values from 0.1 to 1.9
- w_in: bfloat16 [16, 4096, 2, 2048], P('ctx', None, None, 'exp'), may hold values from -0.09375 to 0.09375
- w_out: bfloat16 [16, 2048, 4096], P('ctx', 'exp'), may hold values from -0.125 to 0.125
- routes: int32 [1024, 8], P('ctx'), may hold values from 0 to 15, all different within a row; in each aligned block of 128 rows (0 to 127, 128 to 255, ...) at most 96 rows name the same one
- gate_weights: float32 [1024, 8], P('ctx'), may hold values from 0.05 to 0.5
- doc_lengths: int32 [12], replicated, may hold values from 1 to 640, 1024 in all
Outputs:
- mixed: bfloat16 [1024, 4096], P('ctx', 'exp')
The draws below stay inside these ranges and needn't reach their ends.
Inputs may be any that keep to these rules, and one draw needn't show every extreme that they name: `routes`: the 128 rows of one index of ctx name each expert at most 96 times in all, a bound that some block reaches.
All inputs are finite; a program needn't handle non-finite values.
Results may differ from the reference program's by a relative error of at most 0.009.
Values may be sent and summed in bfloat16 or wider, within the bound.
A program may use at most 128 MiB of HBM per device.

```python
import math
import jax
import jax.numpy as jnp
import numpy as np
from jax import lax

D = 4096
HEADS = 64
NOPE = 128
ROPE = 64
LAT = 512
VDIM = 128
FF = 2048
TOP = 8
DOCS = 12
TOK = 128
SEQ = 1024
EXPERTS = 16
CAP = 96
LONGEST = 640
N_CTX = 8
N_EXP = 4


def draw_latent(key, part):
    key = jax.random.fold_in(key, 11)
    base = jnp.clip(jax.random.normal(key, (SEQ, LAT + ROPE), jnp.float32), -8.0, 8.0)
    return base.astype(jnp.bfloat16)


def draw_query(key, part):
    key = jax.random.fold_in(key, 12)
    base = jnp.clip(jax.random.normal(key, (SEQ, HEADS, NOPE + ROPE), jnp.float32), -8.0, 8.0)
    return base.reshape(SEQ, HEADS * (NOPE + ROPE)).astype(jnp.bfloat16)


def feature_scales(key, low, ratio):
    ramp = jnp.arange(D, dtype=jnp.float32) / D
    jitter = jax.random.uniform(jax.random.fold_in(key, 5), (D,), jnp.float32, 0.7, 1.4)
    return low * jnp.power(ratio, ramp) * jitter


def draw_residual(key, part):
    key = jax.random.fold_in(key, 13)
    scales = feature_scales(key, 0.3, 10.0)
    base = jnp.clip(jax.random.normal(key, (SEQ, D), jnp.float32), -3.5, 3.5)
    return jnp.clip(base * scales[None, :], -16.0, 16.0).astype(jnp.bfloat16)


def level_of(stream_key, extent, shards, low, high):
    level, own = 1.0, jax.random.fold_in(stream_key, 6)
    for axis_at, parts in shards:
        draws = jnp.exp(jax.random.uniform(jax.random.fold_in(own, axis_at), (parts,), jnp.float32, low / len(shards), high / len(shards)))
        level = level * jnp.repeat(draws, extent[axis_at] // parts).reshape([-1 if axis == axis_at else 1 for axis in range(len(extent))])
    return level


def split_up(count, total, most, lean):
    weights = [(1 << 20) // math.isqrt(standing ** lean) + 1 for standing in range(2, count + 1)]
    rest, holding = total - most - (count - 1), [1] * (count - 1)
    while rest > 0:
        free = [i for i in range(count - 1) if holding[i] < most]
        whole, remaining = sum([weights[i] for i in free]), rest
        for i in free:
            addition = min(most - holding[i], max(1, remaining * weights[i] // whole), rest)
            holding[i] = holding[i] + addition
            rest = rest - addition
    return np.array([most] + holding)


def uneven(key, count, total, bound, skew):
    if count == 2:
        one = jax.random.randint(key, (), max(1, total - bound), min(bound, total - 1) + 1)
        return jnp.stack([one, total - one])
    sizes = jnp.asarray(split_up(count, total, bound, skew), jnp.int32)
    twos = (count - 1) // 2
    donor, receiver = sizes[1:1 + 2 * twos:2], sizes[2:2 + 2 * twos:2]
    slack = jnp.minimum(donor - 1, bound - receiver)
    shifted = jax.random.randint(jax.random.fold_in(key, 1), (twos,), 0, 1 << 20) % (slack + 1)
    sizes = sizes.at[1:1 + 2 * twos:2].set(donor - shifted).at[2:2 + 2 * twos:2].set(receiver + shifted)
    return sizes[jax.random.permutation(jax.random.fold_in(key, 2), count)]


def shared_out(stream_key, own, number, rows, number_of, top, bound, skew):
    ranking = jax.random.permutation(stream_key, number_of)
    heavy_load, ordinary = load_shares(number_of, rows * top, bound, skew, True), load_shares(number_of, rows * top, bound, skew, False)
    places = jnp.arange(number_of)

    def named(lengths, offset_by):
        used = int((lengths > 0).sum())
        fixed = max(1, used // 4)
        moved = fixed + (places - fixed + offset_by * (used - fixed)) % max(1, number_of - fixed)
        return jnp.zeros((number_of,), jnp.int32).at[ranking[jnp.where(places < fixed, places, moved)]].set(jnp.asarray(lengths, jnp.int32))

    lengths = jnp.where(number % 4 == 0, named(heavy_load, number // 4), named(ordinary, number - number // 4 - 1))
    mixed = jax.random.permutation(jax.random.fold_in(own, 3), number_of)
    donor, receiver = mixed[0:number_of // 2 * 2:2], mixed[1:number_of // 2 * 2:2]
    slack = jnp.minimum(lengths[donor] - 1, bound - lengths[receiver]) // 2
    slack = jnp.where((donor == ranking[0]) | (receiver == ranking[0]) | (lengths[receiver] == 0), 0, jnp.maximum(slack, 0))
    moved = jax.random.randint(jax.random.fold_in(own, 4), (number_of // 2,), 0, 1 << 20) % (slack + 1)
    lengths = lengths.at[donor].add(-moved).at[receiver].add(moved)
    items = jnp.searchsorted(jnp.cumsum(lengths), jnp.arange(rows * top), side="right").astype(jnp.int32)
    grid = items.reshape(top, rows).T
    grid = grid[jax.random.permutation(jax.random.fold_in(own, 1), rows)]
    offset_by = jax.random.randint(jax.random.fold_in(own, 2), (rows, 1), 0, top)
    return jnp.take_along_axis(grid, (jnp.arange(top)[None, :] + offset_by) % top, axis=1)


def load_shares(number_of, total, bound, skew, full):
    loads = [(1 << 20) // math.isqrt(grade ** skew) + 1 for grade in range(1, number_of + 1)]
    largest = bound if full else min(bound, max(-(-total // number_of), total * loads[0] // sum(loads)))
    least = 1 if total - largest >= number_of - 1 else 0
    holding, surplus = [largest] + [least] * (number_of - 1), total - largest - least * (number_of - 1)
    while surplus > 0:
        free = [i for i in range(1, number_of) if holding[i] < largest] or [i for i in range(1, number_of) if holding[i] < bound]
        whole, left = sum([loads[i] for i in free]), surplus
        for i in free:
            extra = min(bound - holding[i], max(1, left * loads[i] // whole), surplus)
            holding[i] = holding[i] + extra
            surplus = surplus - extra
    return np.array(holding)


def scatter_about(key, dims, scale, bound, split=(), held_as=jnp.bfloat16):
    values = scale * jax.random.normal(key, dims, jnp.float32)
    if split:
        values = values * level_of(key, dims, split, -0.22, 0.18)
    return jnp.clip(values, -bound, bound).astype(held_as)


def setup_inputs(seed: int = 0) -> dict:
    key_list = jax.random.split(jax.random.key(seed), 13)
    latent = draw_latent(jax.random.fold_in(key_list[12], 71), 0)
    query = draw_query(jax.random.fold_in(key_list[12], 71), 0)
    w_uk = scatter_about(key_list[2], (HEADS, LAT, NOPE), NOPE ** -0.5, 0.5, ((0, 4),))
    w_uv = scatter_about(key_list[3], (HEADS, LAT, VDIM), LAT ** -0.5, 0.25, ((0, 4),))
    w_o = scatter_about(key_list[4], (HEADS * VDIM, D), (HEADS * VDIM) ** -0.5, 0.0625, ((0, 4),))
    residual = draw_residual(jax.random.fold_in(key_list[12], 71), 0)
    norm_gain = jnp.clip(1.0 + 0.18 * jax.random.normal(key_list[6], (D,), jnp.float32), 0.1, 1.9)
    w_in = scatter_about(key_list[7], (EXPERTS, D, 2, FF), D ** -0.5, 0.09375, ((0, 8), (3, 4)))
    w_out = scatter_about(key_list[8], (EXPERTS, FF, D), FF ** -0.5, 0.125, ((0, 8), (1, 4)))
    routes_keys = jax.random.split(jax.random.fold_in(key_list[9], 1), SEQ // TOK)
    routes_turns = jax.random.permutation(jax.random.fold_in(key_list[9], 3), SEQ // TOK)
    routes = jax.vmap(lambda own, number: shared_out(jax.random.fold_in(key_list[9], 2), own, number, TOK, EXPERTS, TOP, CAP, 2))(routes_keys, routes_turns).reshape((SEQ, TOP))
    gate_weights = jnp.clip(jnp.exp(math.log(0.5) - 2.3025851 * jax.random.uniform(key_list[10], (SEQ, TOP), jnp.float32) ** level_of(key_list[10], (SEQ, TOP), ((0, 8),), -0.2, 0.2)), 0.05, 0.5)
    doc_lengths = uneven(key_list[11], DOCS, SEQ, LONGEST, 2).astype(jnp.int32)
    return dict(latent=latent, query=query, w_uk=w_uk, w_uv=w_uv, w_o=w_o, residual=residual, norm_gain=norm_gain, w_in=w_in, w_out=w_out, routes=routes, gate_weights=gate_weights, doc_lengths=doc_lengths)


def reference(latent, query, w_uk, w_uv, w_o, residual, norm_gain, w_in, w_out, routes, gate_weights, doc_lengths):
    score_scale = 1.0 / math.sqrt(NOPE + ROPE)
    positions = jnp.arange(SEQ, dtype=jnp.int32)
    doc_ends = jnp.cumsum(doc_lengths)
    doc_ids = lax.optimization_barrier(jnp.sum((positions[:, None] >= doc_ends[None, :]).astype(jnp.int32), axis=1))
    allowed = (doc_ids[:, None] == doc_ids[None, :]) & (positions[:, None] >= positions[None, :])
    q_heads = query.reshape(SEQ, HEADS, NOPE + ROPE).transpose(1, 0, 2)
    value_rows = latent[:, :LAT]

    def one_head(inputs):
        q_head, key_up, value_up = inputs
        q_lat = jnp.dot(q_head[:, :NOPE], key_up.T, preferred_element_type=jnp.float32).astype(jnp.bfloat16)
        q_full = jnp.concatenate([q_lat, q_head[:, NOPE:]], axis=1)
        scores = jnp.dot(q_full, latent.T, preferred_element_type=jnp.float32) * score_scale
        scores = jnp.where(allowed, scores, -1e+30)
        row_max = lax.optimization_barrier(jnp.max(scores, axis=1, keepdims=True))
        weights = jnp.where(allowed, jnp.exp(scores - row_max), 0.0)
        row_total = lax.optimization_barrier(jnp.sum(weights, axis=1))
        o_lat = (jnp.dot(weights.astype(jnp.bfloat16), value_rows, preferred_element_type=jnp.float32) / row_total[:, None]).astype(jnp.bfloat16)
        return jnp.dot(o_lat, value_up, preferred_element_type=jnp.float32).astype(jnp.bfloat16)
    head_stack = lax.map(one_head, (q_heads, w_uk, w_uv))
    head_out = head_stack.transpose(1, 0, 2).reshape(SEQ, HEADS * VDIM)
    hidden = residual.astype(jnp.float32) + jnp.dot(head_out, w_o, preferred_element_type=jnp.float32)
    mean_sq = lax.optimization_barrier(jnp.mean(hidden * hidden, axis=1, keepdims=True))
    normed = (hidden * lax.rsqrt(mean_sq + 1e-06) * norm_gain.astype(jnp.float32)).astype(jnp.bfloat16)
    row_limit = N_CTX * CAP

    def expert_step(moe_sum, inputs):
        expert_id, expert_in, expert_out = inputs
        hit_mask = routes == expert_id
        weight = lax.optimization_barrier(jnp.sum(jnp.where(hit_mask, gate_weights, 0.0), axis=1))
        chosen = jnp.any(hit_mask, axis=1)
        row_ids = jnp.nonzero(chosen, size=row_limit, fill_value=0)[0].astype(jnp.int32)
        live_rows = (jnp.arange(row_limit, dtype=jnp.int32) < jnp.sum(chosen.astype(jnp.int32))).astype(jnp.float32)
        picked_rows = normed[row_ids].astype(jnp.float32)
        hidden_pre = jnp.einsum('md,dgf->mgf', picked_rows, expert_in.astype(jnp.float32))
        activated = (jax.nn.silu(hidden_pre[:, 0]) * hidden_pre[:, 1]).astype(jnp.bfloat16)
        act_blocks = activated.reshape(row_limit, N_EXP, FF // N_EXP).astype(jnp.float32)
        down_blocks = expert_out.reshape(N_EXP, FF // N_EXP, D).astype(jnp.float32)
        partials = jnp.einsum('mbf,bfd->mbd', act_blocks, down_blocks).astype(jnp.bfloat16)
        block_sum = lax.optimization_barrier(jnp.sum(partials.astype(jnp.float32), axis=1))
        contrib = block_sum * (weight[row_ids] * live_rows)[:, None]
        return (moe_sum.at[row_ids].add(contrib), None)
    moe_out, _ = lax.scan(expert_step, jnp.zeros((SEQ, D), jnp.float32), (jnp.arange(EXPERTS, dtype=jnp.int32), w_in, w_out))
    return (hidden + moe_out).astype(jnp.bfloat16)
```

```python
import math

import jax
import jax.numpy as jnp
from jax import lax
from jax.sharding import PartitionSpec as P

D = 4096
NOPE = 128
ROPE = 64
LAT = 512
VDIM = 128
TOP = 8


epsilon = 1e-06


def document(positions, doc_ends):
    return jnp.sum((positions[:, None] >= doc_ends[None, :]).astype(jnp.int32), axis=1)


def expert_gates(routes, gate_weights, first_expert, local_experts):
    named = first_expert + jnp.arange(local_experts, dtype=jnp.int32)
    hit = routes[:, :, None] == named[None, None, :]
    return jnp.sum(jnp.where(hit, gate_weights[:, :, None], 0.0), axis=1)


def expert_mlp(rows, inverse, gates, w_in, w_out):
    experts, _, _, units = w_in.shape
    hidden_pre = jnp.einsum("td,edgf->tegf", rows, w_in, preferred_element_type=jnp.float32)
    hidden_pre = hidden_pre * inverse[:, None, None, None]
    activated = jax.nn.silu(hidden_pre[:, :, 0, :]) * hidden_pre[:, :, 1, :] * gates[:, :, None]
    activated = activated.astype(jnp.bfloat16).reshape(rows.shape[0], experts * units)
    return jnp.dot(
        activated, w_out.reshape(experts * units, w_out.shape[2]), preferred_element_type=jnp.float32
    ).astype(jnp.bfloat16)


def body(
    latent,
    query,
    w_uk,
    w_uv,
    w_o,
    residual,
    norm_gain,
    w_in,
    w_out,
    routes,
    gate_weights,
    doc_lengths,
):
    tokens = latent.shape[0]
    heads = w_uk.shape[0]
    qk_width = NOPE + ROPE
    score_scale = 1.0 / math.sqrt(qk_width)
    doc_ends = jnp.cumsum(doc_lengths)
    first_pos = lax.axis_index("ctx") * tokens
    q_pos = first_pos + jnp.arange(tokens, dtype=jnp.int32)
    q_doc = document(q_pos, doc_ends)
    q_rows = query.reshape(tokens, heads, qk_width)
    q_lat = jnp.einsum(
        "thn,hln->htl", q_rows[:, :, :NOPE], w_uk, preferred_element_type=jnp.float32
    ).astype(jnp.bfloat16)
    q_full = jnp.concatenate(
        [q_lat, jnp.transpose(q_rows[:, :, NOPE:], (1, 0, 2))], axis=2
    ).reshape(heads * tokens, LAT + ROPE)
    row_pos = jnp.tile(q_pos, heads)
    row_doc = jnp.tile(q_doc, heads)
    row_count = heads * tokens
    piece = lax.all_gather(latent, "ctx", axis=0, tiled=True)
    all_routes = lax.all_gather(routes, "ctx", axis=0, tiled=True)
    all_gates = lax.all_gather(gate_weights, "ctx", axis=0, tiled=True)
    key_pos = jnp.arange(piece.shape[0], dtype=jnp.int32)
    key_doc = document(key_pos, doc_ends)
    allowed = (row_doc[:, None] == key_doc[None, :]) & (row_pos[:, None] >= key_pos[None, :])
    row_max = jnp.full((row_count,), -1e30, jnp.float32)
    scores = jnp.dot(q_full, piece.T, preferred_element_type=jnp.float32) * score_scale
    scores = jnp.where(allowed, scores, -1e30)
    new_max = jnp.maximum(row_max, jnp.max(scores, axis=1))
    weights = jnp.where(allowed, jnp.exp(scores - new_max[:, None]), 0.0)
    row_total = jnp.sum(weights, axis=1)
    accumulated = jnp.dot(
        weights.astype(jnp.bfloat16), piece[:, :LAT], preferred_element_type=jnp.float32
    )
    row_max, row_total, accumulated = (new_max, row_total, accumulated)
    o_lat = (accumulated / row_total[:, None]).astype(jnp.bfloat16).reshape(heads, tokens, LAT)
    head_out = (
        jnp.einsum("htl,hlv->thv", o_lat, w_uv, preferred_element_type=jnp.float32)
        .astype(jnp.bfloat16)
        .reshape(tokens, heads * VDIM)
    )
    local_width = residual.shape[1]
    attn_t = lax.psum_scatter(
        lax.dot_general(
            w_o, head_out, (((0,), (1,)), ((), ())), preferred_element_type=jnp.float32
        ).astype(jnp.bfloat16),
        "exp",
        scatter_dimension=0,
        tiled=True,
    ).astype(jnp.float32)
    hidden = residual.astype(jnp.float32) + attn_t.T
    squares = lax.psum(jnp.sum(hidden * hidden, axis=1), "exp")
    inverse = lax.all_gather(lax.rsqrt(squares / D + epsilon), "ctx", axis=0, tiled=True)
    local_experts = w_in.shape[0]
    first_expert = lax.axis_index("ctx") * local_experts
    scaled = (hidden * norm_gain[None, :]).astype(jnp.bfloat16)
    rows = lax.all_gather(scaled, "exp", axis=1, tiled=True)
    rows = lax.all_gather(rows, "ctx", axis=0, tiled=True)
    gates = expert_gates(all_routes, all_gates, first_expert, local_experts)
    mixed = expert_mlp(rows, inverse, gates, w_in, w_out)
    mixed = lax.psum_scatter(mixed, "ctx", scatter_dimension=0, tiled=True)
    mixed = lax.psum_scatter(mixed, "exp", scatter_dimension=1, tiled=True)
    return (hidden + mixed.astype(jnp.float32)).astype(jnp.bfloat16)


def solution(mesh):
    placed = (
        P("ctx", None),
        P("ctx", "exp"),
        P("exp", None, None),
        P("exp", None, None),
        P("exp", None),
        P("ctx", "exp"),
        P("exp"),
        P("ctx", None, None, "exp"),
        P("ctx", "exp", None),
        P("ctx", None),
        P("ctx", None),
        P(),
    )
    return jax.shard_map(
        body, mesh=mesh, in_specs=placed, out_specs=P("ctx", "exp"), check_vma=False
    )
```

```python
import functools
import math

import jax
import jax.numpy as jnp
from jax import lax
from jax.experimental import pallas as pl
from jax.experimental.pallas import tpu as pltpu
from jax.sharding import PartitionSpec as P

D = 4096
NOPE = 128
ROPE = 64
LAT = 512
VDIM = 128
TOP = 8


epsilon = 1e-06


def document(positions, doc_ends):
    return jnp.sum((positions[:, None] >= doc_ends[None, :]).astype(jnp.int32), axis=1)


MESH = pl.DeviceIdType.MESH


def ring_place(chip, chips):
    half = chips // 2
    return chip + (chip // half) * (chips - 1 + half - 2 * chip)


def ring_member(place, chips, core):
    return ring_place(lax.rem(place + chips, chips), chips) * 2 + core


def by_distance(count):
    return sorted(range(count), key=lambda step: min(step, count - step))


def greet(peers):
    barrier = pltpu.get_barrier_semaphore()
    for peer in peers:
        pl.semaphore_signal(barrier, inc=1, device_id=peer, device_id_type=MESH)
    pl.semaphore_wait(barrier, len(peers))


def neighbours(chips, count_exp):
    ctx, exp = lax.axis_index("ctx"), lax.axis_index("exp")
    core = lax.rem(ctx, 2)
    place = ring_place(ctx // 2, chips)
    sibling = (ctx + 1 - 2 * core, exp)
    right = (ring_member(place + 1, chips, core), exp)
    left = (ring_member(place - 1, chips, core), exp)
    across = [(ctx, lax.rem(exp + step, count_exp)) for step in range(count_exp)]
    return ctx, exp, core, place, sibling, (right, left), across


def gather_kernel(chips, count_exp, with_extra, *refs):
    if with_extra:
        own_ref, extra_ref, out_ref, extra_out = refs[:4]
        refs = refs[4:]
    else:
        own_ref, out_ref = refs[:2]
        extra_ref = extra_out = None
        refs = refs[2:]
    local_sem, z_send, z_recv, ring_send, ring_recv, sib_send, sib_recv = refs
    ctx, exp, core, place, sibling, sides, across = neighbours(chips, count_exp)
    half = chips // 2
    rows, cols = own_ref.shape
    chunks = by_distance(count_exp) + (["extra"] if with_extra else [])
    slot_of = {chunk: at for at, chunk in enumerate(chunks)}
    greet([*across[1:], *sides, sibling])

    def block(owner, chunk, part):
        if chunk == "extra":
            height = extra_ref.shape[0] * count_exp
            return extra_out.at[pl.ds(pl.multiple_of(owner * height, height), height)]
        start, height = (0, rows) if part is None else (part * (rows // 2), rows // 2)
        down = pl.ds(pl.multiple_of(owner * rows + start, rows // 2), height)
        if count_exp == 1:
            return out_ref.at[down]
        column = lax.rem(exp - chunk + count_exp, count_exp) * cols
        return out_ref.at[down, pl.ds(pl.multiple_of(column, cols), cols)]

    def extra_block(which):
        height = extra_ref.shape[0]
        at = (ctx * count_exp + which) * height
        return extra_out.at[pl.ds(pl.multiple_of(at, height), height)]

    started = []

    def send(source, target, sems, at, device):
        copy = pltpu.make_async_remote_copy(
            src_ref=source,
            dst_ref=target,
            send_sem=sems[0].at[at],
            recv_sem=sems[1].at[at],
            device_id=device,
            device_id_type=MESH,
        )
        copy.start()
        started.append(copy)
        return copy

    keeps = [pltpu.make_async_copy(own_ref, block(ctx, 0, None), local_sem.at[0])]
    if with_extra:
        keeps.append(pltpu.make_async_copy(extra_ref, extra_block(exp), local_sem.at[1]))
    for keep in keeps:
        keep.start()
    arriving = {}
    z_sems = (z_send, z_recv)
    for step in range(1, count_exp):
        if with_extra:
            arriving["extra", step] = send(
                extra_ref, extra_block(exp), z_sems, count_exp + step, across[step]
            )
    for step in by_distance(count_exp)[1:]:
        arriving[step] = send(own_ref, block(ctx, 0, None), z_sems, step, across[step])
    for keep in keeps:
        keep.wait()

    ring_sems, sib_sems = (ring_send, ring_recv), (sib_send, sib_recv)
    ring, sib = {}, []

    def share(owner, chunk, part, at):
        piece = block(owner, chunk, part)
        sib.append(send(piece, piece, sib_sems, at, sibling))

    def hop_on(chunk, hop, side):
        if chunk == "extra" and hop == half and side == 1:
            return
        part = side if hop == half and chunk != "extra" else None
        source = ring_member(place - (hop - 1) * (1 - 2 * side), chips, core)
        piece = block(source, chunk, part)
        at = (side * half + hop - 1) * len(chunks) + slot_of[chunk]
        ring[chunk, hop, side] = send(piece, piece, ring_sems, at, sides[side])

    def arrive(chunk, hop):
        for side in range(2):
            if (chunk, hop, side) not in ring:
                continue
            ring[chunk, hop, side].wait_recv()
            if hop < half:
                hop_on(chunk, hop + 1, side)
        for side in range(2):
            if (chunk, hop, side) not in ring:
                continue
            part = side if hop == half and chunk != "extra" else None
            source = ring_member(place - hop * (1 - 2 * side), chips, core)
            at = len(chunks) + (side * half + hop - 1) * len(chunks) + slot_of[chunk]
            share(source, chunk, part, at)

    for turn in range(len(chunks) + half):
        if turn < len(chunks):
            chunk = chunks[turn]
            if chunk == "extra":
                for step in range(1, count_exp):
                    arriving["extra", step].wait_recv()
            elif chunk != 0:
                arriving[chunk].wait_recv()
            for side in range(2):
                hop_on(chunk, 1, side)
            share(ctx, chunk, None, slot_of[chunk])
        for hop in range(1, half + 1):
            if 0 <= turn - hop < len(chunks):
                arrive(chunks[turn - hop], hop)
    for copy in sib:
        copy.wait_recv()
    for copy in started:
        copy.wait_send()


def gather(count_ctx, count_exp, own, extra, collective_id):
    chips = count_ctx // 2
    half = chips // 2
    rows, cols = own.shape
    outs = [jax.ShapeDtypeStruct((count_ctx * rows, count_exp * cols), own.dtype)]
    operands = [own]
    if extra is not None:
        operands.append(extra)
        outs.append(
            jax.ShapeDtypeStruct((count_ctx * count_exp * extra.shape[0], extra.shape[1]), extra.dtype)
        )
    chunks = count_exp + len(operands) - 1
    dma = pltpu.SemaphoreType.DMA
    result = pl.pallas_call(
        functools.partial(gather_kernel, chips, count_exp, extra is not None),
        out_shape=outs,
        in_specs=[pl.BlockSpec(memory_space=pl.ANY)] * len(operands),
        out_specs=[pl.BlockSpec(memory_space=pl.ANY)] * len(outs),
        scratch_shapes=[
            dma((2,)),
            dma((2 * count_exp,)),
            dma((2 * count_exp,)),
            dma((2 * half * chunks,)),
            dma((2 * half * chunks,)),
            dma(((2 * half + 1) * chunks,)),
            dma(((2 * half + 1) * chunks,)),
        ],
        compiler_params=pltpu.CompilerParams(collective_id=collective_id, has_side_effects=True),
    )(*operands)
    return result if extra is not None else result[0]


def scatter_kernel(
    chips, count_exp, sums_ref, out_ref, held, passed, landed, leaving, returned,
    load_sem, sib_send, sib_recv, ring_send, ring_recv, z_send, z_recv,
):
    ctx, exp, core, place, sibling, sides, across = neighbours(chips, count_exp)
    half = chips // 2
    rows, cols = out_ref.shape
    order = by_distance(count_exp)[::-1]
    greet([*across[1:], *sides, sibling])

    def block(owner, chunk):
        column = across[chunk][1] * cols
        return sums_ref.at[
            pl.ds(pl.multiple_of(owner * rows, rows), rows),
            pl.ds(pl.multiple_of(column, cols), cols),
        ]

    started = []

    def send(source, target, sems, at, device):
        copy = pltpu.make_async_remote_copy(
            src_ref=source,
            dst_ref=target,
            send_sem=sems[0].at[at],
            recv_sem=sems[1].at[at],
            device_id=device,
            device_id_type=MESH,
        )
        copy.start()
        started.append(copy)
        return copy

    loads, swaps = {}, {}
    offsets = sorted(range(chips), key=lambda offset: -min(offset, chips - offset))
    for chunk in order:
        for offset in offsets:
            at = offset * count_exp + chunk
            theirs = ring_member(place + offset, chips, 1 - core)
            mine = ring_member(place + offset, chips, core)
            swaps[offset, chunk] = send(
                block(theirs, chunk), passed.at[at], (sib_send, sib_recv), at, sibling
            )
            loads[offset, chunk] = pltpu.make_async_copy(
                block(mine, chunk), held.at[at], load_sem.at[at]
            )
            loads[offset, chunk].start()

    def pair(offset, chunk):
        loads[offset, chunk].wait()
        swaps[offset, chunk].wait_recv()
        at = offset * count_exp + chunk
        return held[at].astype(jnp.float32) + passed[at].astype(jnp.float32)

    ring = {}
    stretch = rows // 2

    def ring_slot(side, step, chunk):
        return (side * half + step - 1) * count_exp + chunk

    def pass_on(offset, side, step, chunk):
        at = offset * count_exp + chunk
        slot = ring_slot(side, step, chunk)
        source, target = held.at[at], landed.at[slot]
        if step == 1:
            source = source.at[pl.ds(side * stretch, stretch)]
            target = target.at[pl.ds(side * stretch, stretch)]
        ring[side, step, chunk] = send(source, target, (ring_send, ring_recv), slot, sides[side])

    def begin(chunk):
        at = half * count_exp + chunk
        held[at] = pair(half, chunk).astype(held.dtype)
        for side in range(2):
            pass_on(half, side, 1, chunk)

    def middle(chunk, step):
        for side in range(2):
            offset = half - step + 1
            offset = offset if side == 0 else chips - offset
            at = offset * count_exp + chunk
            held[at] = pair(offset, chunk).astype(held.dtype)
            ring[side, step - 1, chunk].wait_recv()
            slot = ring_slot(side, step - 1, chunk)
            part = pl.ds(side * stretch, stretch) if step == 2 else pl.ds(0, rows)
            held[at, part] = (
                held[at, part].astype(jnp.float32) + landed[slot, part].astype(jnp.float32)
            ).astype(held.dtype)
            pass_on(offset, side, step, chunk)

    back = {}

    def finish(chunk):
        total = pair(0, chunk)
        for side in range(2):
            ring[side, half, chunk].wait_recv()
            total += landed[ring_slot(side, half, chunk)].astype(jnp.float32)
        if chunk == 0:
            out_ref[...] = total
        else:
            leaving[chunk] = total.astype(leaving.dtype)
            back[chunk] = send(
                leaving.at[chunk], returned.at[chunk], (z_send, z_recv), chunk, across[chunk]
            )

    for turn in range(count_exp + half):
        if turn < count_exp:
            begin(order[turn])
        for step in range(2, half + 1):
            if 0 <= turn - step + 1 < count_exp:
                middle(order[turn - step + 1], step)
        if 0 <= turn - half < count_exp:
            finish(order[turn - half])
    total = out_ref[...]
    for chunk in order[:-1]:
        back[chunk].wait_recv()
        total += returned[chunk].astype(jnp.float32)
    out_ref[...] = total
    for copy in started:
        copy.wait_send()


def scatter(count_ctx, count_exp, sums, collective_id):
    chips = count_ctx // 2
    half = chips // 2
    rows, cols = sums.shape[0] // count_ctx, sums.shape[1] // count_exp
    dma = pltpu.SemaphoreType.DMA
    blocks, hops = chips * count_exp, 2 * half * count_exp
    return pl.pallas_call(
        functools.partial(scatter_kernel, chips, count_exp),
        out_shape=jax.ShapeDtypeStruct((rows, cols), jnp.float32),
        in_specs=[pl.BlockSpec(memory_space=pl.ANY)],
        out_specs=pl.BlockSpec(memory_space=pltpu.VMEM),
        scratch_shapes=[
            pltpu.VMEM((blocks, rows, cols), sums.dtype),
            pltpu.VMEM((blocks, rows, cols), sums.dtype),
            pltpu.VMEM((hops, rows, cols), sums.dtype),
            pltpu.VMEM((count_exp, rows, cols), sums.dtype),
            pltpu.VMEM((count_exp, rows, cols), sums.dtype),
            dma((blocks,)),
            dma((blocks,)),
            dma((blocks,)),
            dma((hops,)),
            dma((hops,)),
            dma((count_exp,)),
            dma((count_exp,)),
        ],
        compiler_params=pltpu.CompilerParams(
            collective_id=collective_id, has_side_effects=True, vmem_limit_bytes=40 * 1024 * 1024
        ),
    )(sums)


def three_terms(values):
    first = lax.reduce_precision(values, 8, 7)
    second = lax.reduce_precision(values - first, 8, 7)
    third = values - first - second
    return [term.astype(jnp.bfloat16) for term in (first, second, third)]


def dense_gates(routes, gate_weights, experts):
    hit = routes[:, :, None] == jnp.arange(experts, dtype=jnp.int32)[None, None, :]
    return jnp.sum(jnp.where(hit, gate_weights[:, :, None], 0.0), axis=1)


def expert_mlp(rows, inverse, gates, w_in, w_out):
    experts, _, _, units = w_in.shape
    hidden_pre = jnp.einsum("td,edgf->tegf", rows, w_in, preferred_element_type=jnp.float32)
    hidden_pre = hidden_pre * inverse[:, None, None, None]
    activated = jax.nn.silu(hidden_pre[:, :, 0, :]) * hidden_pre[:, :, 1, :] * gates[:, :, None]
    activated = activated.astype(jnp.bfloat16).reshape(rows.shape[0], experts * units)
    return jnp.dot(
        activated, w_out.reshape(experts * units, w_out.shape[2]), preferred_element_type=jnp.float32
    ).astype(jnp.bfloat16)


def body(
    latent,
    query,
    w_uk,
    w_uv,
    w_o,
    residual,
    norm_gain,
    w_in,
    w_out,
    routes,
    gate_weights,
    doc_lengths,
):
    count_ctx, count_exp = lax.axis_size("ctx"), lax.axis_size("exp")
    tokens = latent.shape[0]
    heads = w_uk.shape[0]
    qk_width = NOPE + ROPE
    score_scale = 1.0 / math.sqrt(qk_width)
    doc_ends = jnp.cumsum(doc_lengths)
    first_pos = lax.axis_index("ctx") * tokens
    q_pos = first_pos + jnp.arange(tokens, dtype=jnp.int32)
    q_doc = document(q_pos, doc_ends)
    q_rows = query.reshape(tokens, heads, qk_width)
    q_lat = jnp.einsum(
        "thn,hln->htl", q_rows[:, :, :NOPE], w_uk, preferred_element_type=jnp.float32
    ).astype(jnp.bfloat16)
    q_full = jnp.concatenate(
        [q_lat, jnp.transpose(q_rows[:, :, NOPE:], (1, 0, 2))], axis=2
    ).reshape(heads * tokens, LAT + ROPE)
    row_pos = jnp.tile(q_pos, heads)
    row_doc = jnp.tile(q_doc, heads)
    row_count = heads * tokens
    local_experts = w_in.shape[0]
    experts = local_experts * count_ctx
    own_gates = three_terms(dense_gates(routes, gate_weights, experts))
    width = LAT + ROPE
    spare = -(width + 3 * experts) % 128
    packed = jnp.concatenate(
        [latent, *own_gates, jnp.zeros((tokens, spare), jnp.bfloat16)], axis=1
    )
    packed = gather(count_ctx, 1, packed, None, 0)
    piece = packed[:, :width]
    all_gates = jnp.sum(
        packed[:, width : width + 3 * experts].astype(jnp.float32).reshape(-1, 3, experts), axis=1
    )
    first_expert = lax.axis_index("ctx") * local_experts
    gates = lax.dynamic_slice_in_dim(all_gates, first_expert, local_experts, axis=1)
    key_pos = jnp.arange(piece.shape[0], dtype=jnp.int32)
    key_doc = document(key_pos, doc_ends)
    allowed = (row_doc[:, None] == key_doc[None, :]) & (row_pos[:, None] >= key_pos[None, :])
    row_max = jnp.full((row_count,), -1e30, jnp.float32)
    scores = jnp.dot(q_full, piece.T, preferred_element_type=jnp.float32) * score_scale
    scores = jnp.where(allowed, scores, -1e30)
    new_max = jnp.maximum(row_max, jnp.max(scores, axis=1))
    weights = jnp.where(allowed, jnp.exp(scores - new_max[:, None]), 0.0)
    row_total = jnp.sum(weights, axis=1)
    accumulated = jnp.dot(
        weights.astype(jnp.bfloat16), piece[:, :LAT], preferred_element_type=jnp.float32
    )
    row_max, row_total, accumulated = (new_max, row_total, accumulated)
    o_lat = (accumulated / row_total[:, None]).astype(jnp.bfloat16).reshape(heads, tokens, LAT)
    head_out = (
        jnp.einsum("htl,hlv->thv", o_lat, w_uv, preferred_element_type=jnp.float32)
        .astype(jnp.bfloat16)
        .reshape(tokens, heads * VDIM)
    )
    local_width = residual.shape[1]
    attn_t = lax.psum_scatter(
        lax.dot_general(
            w_o, head_out, (((0,), (1,)), ((), ())), preferred_element_type=jnp.float32
        ).astype(jnp.bfloat16),
        "exp",
        scatter_dimension=0,
        tiled=True,
    ).astype(jnp.float32)
    hidden = residual.astype(jnp.float32) + attn_t.T
    squares = jnp.sum(hidden * hidden, axis=1)
    scaled = (hidden * norm_gain[None, :]).astype(jnp.bfloat16)
    rows, squares = gather(
        count_ctx, count_exp, scaled, jnp.broadcast_to(squares[None, :], (8, tokens)), 1
    )
    squares = jnp.sum(squares.reshape(count_ctx, count_exp, 8, tokens)[:, :, 0], axis=1)
    inverse = lax.rsqrt(squares.reshape(-1) / D + epsilon)
    mixed = scatter(count_ctx, count_exp, expert_mlp(rows, inverse, gates, w_in, w_out), 2)
    return (hidden + mixed).astype(jnp.bfloat16)


def solution(mesh):
    placed = (
        P("ctx", None),
        P("ctx", "exp"),
        P("exp", None, None),
        P("exp", None, None),
        P("exp", None),
        P("ctx", "exp"),
        P("exp"),
        P("ctx", None, None, "exp"),
        P("ctx", "exp", None),
        P("ctx", None),
        P("ctx", None),
        P(),
    )
    return jax.shard_map(
        body, mesh=mesh, in_specs=placed, out_specs=P("ctx", "exp"), check_vma=False
    )
```

```python
import functools
import math

import jax
import jax.numpy as jnp
from jax import lax
from jax.experimental import pallas as pl
from jax.experimental.pallas import tpu as pltpu
from jax.sharding import PartitionSpec as P

D = 4096
NOPE = 128
ROPE = 64
LAT = 512
VDIM = 128
TOP = 8


epsilon = 1e-06


def document(positions, doc_ends):
    return jnp.sum((positions[:, None] >= doc_ends[None, :]).astype(jnp.int32), axis=1)


MESH = pl.DeviceIdType.MESH


def ring_place(chip, chips):
    half = chips // 2
    return chip + (chip // half) * (chips - 1 + half - 2 * chip)


def ring_member(place, chips, core):
    return ring_place(lax.rem(place + chips, chips), chips) * 2 + core


def by_distance(count):
    return sorted(range(count), key=lambda step: min(step, count - step))


def greet(peers):
    barrier = pltpu.get_barrier_semaphore()
    for peer in peers:
        pl.semaphore_signal(barrier, inc=1, device_id=peer, device_id_type=MESH)
    pl.semaphore_wait(barrier, len(peers))


def neighbours(chips, count_exp):
    ctx, exp = lax.axis_index("ctx"), lax.axis_index("exp")
    core = lax.rem(ctx, 2)
    place = ring_place(ctx // 2, chips)
    sibling = (ctx + 1 - 2 * core, exp)
    right = (ring_member(place + 1, chips, core), exp)
    left = (ring_member(place - 1, chips, core), exp)
    across = [(ctx, lax.rem(exp + step, count_exp)) for step in range(count_exp)]
    return ctx, exp, core, place, sibling, (right, left), across


def gather_kernel(chips, count_exp, with_extra, *refs):
    if with_extra:
        own_ref, extra_ref, weight_ref, product_ref, extra_out, out_ref, weight, weight_sem = refs[:8]
        refs = refs[8:]
    else:
        own_ref, out_ref = refs[:2]
        extra_ref = extra_out = None
        refs = refs[2:]
    local_sem, z_send, z_recv, ring_send, ring_recv, sib_send, sib_recv = refs
    ctx, exp, core, place, sibling, sides, across = neighbours(chips, count_exp)
    half = chips // 2
    rows, cols = own_ref.shape
    chunks = by_distance(count_exp) + (["extra"] if with_extra else [])
    slot_of = {chunk: at for at, chunk in enumerate(chunks)}
    greet([*across[1:], *sides, sibling])

    def block(owner, chunk, part):
        if chunk == "extra":
            height = extra_ref.shape[0] * count_exp
            return extra_out.at[pl.ds(pl.multiple_of(owner * height, height), height)]
        start, height = (0, rows) if part is None else (part * (rows // 2), rows // 2)
        down = pl.ds(pl.multiple_of(owner * rows + start, rows // 2), height)
        if count_exp == 1:
            return out_ref.at[down]
        column = lax.rem(exp - chunk + count_exp, count_exp) * cols
        return out_ref.at[down, pl.ds(pl.multiple_of(column, cols), cols)]

    def extra_block(which):
        height = extra_ref.shape[0]
        at = (ctx * count_exp + which) * height
        return extra_out.at[pl.ds(pl.multiple_of(at, height), height)]

    started = []

    def send(source, target, sems, at, device):
        copy = pltpu.make_async_remote_copy(
            src_ref=source,
            dst_ref=target,
            send_sem=sems[0].at[at],
            recv_sem=sems[1].at[at],
            device_id=device,
            device_id_type=MESH,
        )
        copy.start()
        started.append(copy)
        return copy

    loads = {}
    if with_extra:
        for chunk in by_distance(count_exp):
            first = lax.rem(exp - chunk + count_exp, count_exp) * cols
            loads[chunk] = pltpu.make_async_copy(
                weight_ref.at[pl.ds(pl.multiple_of(first, cols), cols)],
                weight.at[chunk],
                weight_sem.at[chunk],
            )

    def multiply(chunk):
        loads[chunk].wait()
        for copy in sib_of[chunk]:
            copy.wait_recv()
        first = lax.rem(exp - chunk + count_exp, count_exp) * cols
        chosen = pl.ds(pl.multiple_of(first, cols), cols)
        tall, wide = 512, 256
        across_tiles = product_ref.shape[1] // wide

        def tile(at, carry):
            down = pl.ds(pl.multiple_of(at // across_tiles * tall, tall), tall)
            side = pl.ds(pl.multiple_of(lax.rem(at, across_tiles) * wide, wide), wide)
            product = jnp.dot(
                out_ref[down, chosen], weight[chunk, :, side], preferred_element_type=jnp.float32
            )
            product_ref[down, side] = product if chunk == 0 else product_ref[down, side] + product
            return carry

        lax.fori_loop(0, product_ref.shape[0] // tall * across_tiles, tile, 0)

    keeps = [pltpu.make_async_copy(own_ref, block(ctx, 0, None), local_sem.at[0])]
    if with_extra:
        keeps.append(pltpu.make_async_copy(extra_ref, extra_block(exp), local_sem.at[1]))
    for keep in keeps:
        keep.start()
    arriving = {}
    z_sems = (z_send, z_recv)
    for step in range(1, count_exp):
        if with_extra:
            arriving["extra", step] = send(
                extra_ref, extra_block(exp), z_sems, count_exp + step, across[step]
            )
    for step in by_distance(count_exp)[1:]:
        arriving[step] = send(own_ref, block(ctx, 0, None), z_sems, step, across[step])
    for chunk in loads:
        loads[chunk].start()
    for keep in keeps:
        keep.wait()

    ring_sems, sib_sems = (ring_send, ring_recv), (sib_send, sib_recv)
    ring, sib_of = {}, {chunk: [] for chunk in chunks}

    def share(owner, chunk, part, at):
        piece = block(owner, chunk, part)
        sib_of[chunk].append(send(piece, piece, sib_sems, at, sibling))

    def hop_on(chunk, hop, side):
        if chunk == "extra" and hop == half and side == 1:
            return
        part = side if hop == half and chunk != "extra" else None
        source = ring_member(place - (hop - 1) * (1 - 2 * side), chips, core)
        piece = block(source, chunk, part)
        at = (side * half + hop - 1) * len(chunks) + slot_of[chunk]
        ring[chunk, hop, side] = send(piece, piece, ring_sems, at, sides[side])

    def arrive(chunk, hop):
        for side in range(2):
            if (chunk, hop, side) not in ring:
                continue
            ring[chunk, hop, side].wait_recv()
            if hop < half:
                hop_on(chunk, hop + 1, side)
        for side in range(2):
            if (chunk, hop, side) not in ring:
                continue
            part = side if hop == half and chunk != "extra" else None
            source = ring_member(place - hop * (1 - 2 * side), chips, core)
            at = len(chunks) + (side * half + hop - 1) * len(chunks) + slot_of[chunk]
            share(source, chunk, part, at)

    for turn in range(len(chunks) + half + 1):
        if turn < len(chunks):
            chunk = chunks[turn]
            if chunk == "extra":
                for step in range(1, count_exp):
                    arriving["extra", step].wait_recv()
            elif chunk != 0:
                arriving[chunk].wait_recv()
            for side in range(2):
                hop_on(chunk, 1, side)
            share(ctx, chunk, None, slot_of[chunk])
        for hop in range(1, half + 1):
            if 0 <= turn - hop < len(chunks):
                arrive(chunks[turn - hop], hop)
        done = turn - half - 1
        if 0 <= done < len(chunks) and chunks[done] in loads:
            multiply(chunks[done])
    for chunk in chunks:
        if chunk not in loads:
            for copy in sib_of[chunk]:
                copy.wait_recv()
    for copy in started:
        copy.wait_send()


def gather(count_ctx, count_exp, own, extra, weight, collective_id):
    chips = count_ctx // 2
    half = chips // 2
    rows, cols = own.shape
    outs = [jax.ShapeDtypeStruct((count_ctx * rows, count_exp * cols), own.dtype)]
    operands = [own]
    place, space, held = pl.ANY, None, []
    dma = pltpu.SemaphoreType.DMA
    if extra is not None:
        operands += [extra, weight]
        held = [
            pltpu.VMEM(outs[0].shape, own.dtype),
            pltpu.VMEM((count_exp, cols, weight.shape[1]), weight.dtype),
            dma((count_exp,)),
        ]
        outs = [jax.ShapeDtypeStruct((count_ctx * rows, weight.shape[1]), jnp.float32)]
        place, space = pltpu.VMEM, 52 * 1024 * 1024
        outs.append(
            jax.ShapeDtypeStruct((count_ctx * count_exp * extra.shape[0], extra.shape[1]), extra.dtype)
        )
    chunks = count_exp + len(outs) - 1
    result = pl.pallas_call(
        functools.partial(gather_kernel, chips, count_exp, extra is not None),
        out_shape=outs,
        in_specs=[pl.BlockSpec(memory_space=pl.ANY)] * len(operands),
        out_specs=[pl.BlockSpec(memory_space=place)] + [pl.BlockSpec(memory_space=pl.ANY)] * (len(outs) - 1),
        scratch_shapes=[
            *held,
            dma((2,)),
            dma((2 * count_exp,)),
            dma((2 * count_exp,)),
            dma((2 * half * chunks,)),
            dma((2 * half * chunks,)),
            dma(((2 * half + 1) * chunks,)),
            dma(((2 * half + 1) * chunks,)),
        ],
        compiler_params=pltpu.CompilerParams(
            collective_id=collective_id, has_side_effects=True, vmem_limit_bytes=space
        ),
    )(*operands)
    return result if extra is not None else result[0]


def scatter_kernel(
    chips, count_exp, rows_ref, weight_ref, out_ref, weight, held, passed, landed, leaving, returned,
    load_sem, sib_send, sib_recv, ring_send, ring_recv, z_send, z_recv,
):
    ctx, exp, core, place, sibling, sides, across = neighbours(chips, count_exp)
    half = chips // 2
    rows, cols = out_ref.shape
    order = by_distance(count_exp)[::-1]
    greet([*across[1:], *sides, sibling])

    def block(owner, chunk):
        return held.at[chunk, pl.ds(pl.multiple_of(owner * rows, rows), rows)]

    started = []

    def send(source, target, sems, at, device):
        copy = pltpu.make_async_remote_copy(
            src_ref=source,
            dst_ref=target,
            send_sem=sems[0].at[at],
            recv_sem=sems[1].at[at],
            device_id=device,
            device_id_type=MESH,
        )
        copy.start()
        started.append(copy)
        return copy

    loads, swaps = {}, {}
    offsets = sorted(range(chips), key=lambda offset: -min(offset, chips - offset))
    for chunk in order:
        column = pl.ds(pl.multiple_of(across[chunk][1] * cols, cols), cols)
        loads[chunk] = pltpu.make_async_copy(
            weight_ref.at[:, column], weight.at[chunk], load_sem.at[chunk]
        )
        loads[chunk].start()

    def multiply(chunk):
        loads[chunk].wait()
        tall, wide = 512, 256
        across_tiles = cols // wide

        def tile(at, carry):
            down = pl.ds(pl.multiple_of(at // across_tiles * tall, tall), tall)
            side = pl.ds(pl.multiple_of(lax.rem(at, across_tiles) * wide, wide), wide)
            held[chunk, down, side] = jnp.dot(
                rows_ref[down], weight[chunk, :, side], preferred_element_type=jnp.float32
            ).astype(held.dtype)
            return carry

        lax.fori_loop(0, rows_ref.shape[0] // tall * across_tiles, tile, 0)
        for offset in offsets:
            at = offset * count_exp + chunk
            theirs = ring_member(place + offset, chips, 1 - core)
            swaps[offset, chunk] = send(
                block(theirs, chunk), passed.at[at], (sib_send, sib_recv), at, sibling
            )

    def mine(offset):
        return pl.multiple_of(ring_member(place + offset, chips, core) * rows, rows)

    def pair(offset, chunk):
        swaps[offset, chunk].wait_recv()
        at = offset * count_exp + chunk
        ours = held[chunk, pl.ds(mine(offset), rows)]
        return ours.astype(jnp.float32) + passed[at].astype(jnp.float32)

    ring = {}
    stretch = rows // 2

    def ring_slot(side, step, chunk):
        return (side * half + step - 1) * count_exp + chunk

    def pass_on(offset, side, step, chunk):
        slot = ring_slot(side, step, chunk)
        start, height = (side * stretch, stretch) if step == 1 else (0, rows)
        source = held.at[chunk, pl.ds(pl.multiple_of(mine(offset) + start, stretch), height)]
        target = landed.at[slot, pl.ds(start, height)]
        ring[side, step, chunk] = send(source, target, (ring_send, ring_recv), slot, sides[side])

    def begin(chunk):
        held[chunk, pl.ds(mine(half), rows)] = pair(half, chunk).astype(held.dtype)
        for side in range(2):
            pass_on(half, side, 1, chunk)

    def middle(chunk, step):
        for side in range(2):
            offset = half - step + 1
            offset = offset if side == 0 else chips - offset
            total = pair(offset, chunk)
            ring[side, step - 1, chunk].wait_recv()
            slot = ring_slot(side, step - 1, chunk)
            if step == 2:
                came = landed[slot, pl.ds(side * stretch, stretch)].astype(jnp.float32)
                parts = [total[:stretch], total[stretch:]]
                parts[side] = parts[side] + came
                for which in range(2):
                    down = pl.ds(pl.multiple_of(mine(offset) + which * stretch, stretch), stretch)
                    held[chunk, down] = parts[which].astype(held.dtype)
            else:
                total = total + landed[slot].astype(jnp.float32)
                held[chunk, pl.ds(mine(offset), rows)] = total.astype(held.dtype)
            pass_on(offset, side, step, chunk)

    back = {}

    def finish(chunk):
        total = pair(0, chunk)
        for side in range(2):
            ring[side, half, chunk].wait_recv()
            total += landed[ring_slot(side, half, chunk)].astype(jnp.float32)
        if chunk == 0:
            out_ref[...] = total
        else:
            leaving[chunk] = total.astype(leaving.dtype)
            back[chunk] = send(
                leaving.at[chunk], returned.at[chunk], (z_send, z_recv), chunk, across[chunk]
            )

    multiply(order[0])
    for turn in range(count_exp + half):
        if turn + 1 < count_exp:
            multiply(order[turn + 1])
        if turn < count_exp:
            begin(order[turn])
        for step in range(2, half + 1):
            if 0 <= turn - step + 1 < count_exp:
                middle(order[turn - step + 1], step)
        if 0 <= turn - half < count_exp:
            finish(order[turn - half])
    total = out_ref[...]
    for chunk in order[:-1]:
        back[chunk].wait_recv()
        total += returned[chunk].astype(jnp.float32)
    out_ref[...] = total
    for copy in started:
        copy.wait_send()


def scatter(count_ctx, count_exp, rows_in, weight, collective_id):
    chips = count_ctx // 2
    half = chips // 2
    rows, cols = rows_in.shape[0] // count_ctx, weight.shape[1] // count_exp
    dma = pltpu.SemaphoreType.DMA
    blocks, hops = chips * count_exp, 2 * half * count_exp
    kind = rows_in.dtype
    return pl.pallas_call(
        functools.partial(scatter_kernel, chips, count_exp),
        out_shape=jax.ShapeDtypeStruct((rows, cols), jnp.float32),
        in_specs=[pl.BlockSpec(memory_space=pltpu.VMEM), pl.BlockSpec(memory_space=pl.ANY)],
        out_specs=pl.BlockSpec(memory_space=pltpu.VMEM),
        scratch_shapes=[
            pltpu.VMEM((count_exp, weight.shape[0], cols), kind),
            pltpu.VMEM((count_exp, rows_in.shape[0], cols), kind),
            pltpu.VMEM((blocks, rows, cols), kind),
            pltpu.VMEM((hops, rows, cols), kind),
            pltpu.VMEM((count_exp, rows, cols), kind),
            pltpu.VMEM((count_exp, rows, cols), kind),
            dma((count_exp,)),
            dma((blocks,)),
            dma((blocks,)),
            dma((hops,)),
            dma((hops,)),
            dma((count_exp,)),
            dma((count_exp,)),
        ],
        compiler_params=pltpu.CompilerParams(
            collective_id=collective_id, has_side_effects=True, vmem_limit_bytes=52 * 1024 * 1024
        ),
    )(rows_in, weight)


def three_terms(values):
    first = lax.reduce_precision(values, 8, 7)
    second = lax.reduce_precision(values - first, 8, 7)
    third = values - first - second
    return [term.astype(jnp.bfloat16) for term in (first, second, third)]


def dense_gates(routes, gate_weights, experts):
    hit = routes[:, :, None] == jnp.arange(experts, dtype=jnp.int32)[None, None, :]
    return jnp.sum(jnp.where(hit, gate_weights[:, :, None], 0.0), axis=1)


def activate(hidden_pre, inverse, gates):
    tokens, experts = gates.shape
    hidden_pre = (hidden_pre * inverse[:, None]).reshape(tokens, experts, 2, -1)
    activated = jax.nn.silu(hidden_pre[:, :, 0]) * hidden_pre[:, :, 1] * gates[:, :, None]
    return activated.astype(jnp.bfloat16).reshape(tokens, -1)


def body(
    latent,
    query,
    w_uk,
    w_uv,
    w_o,
    residual,
    norm_gain,
    w_in,
    w_out,
    routes,
    gate_weights,
    doc_lengths,
):
    count_ctx, count_exp = lax.axis_size("ctx"), lax.axis_size("exp")
    tokens = latent.shape[0]
    heads = w_uk.shape[0]
    qk_width = NOPE + ROPE
    score_scale = 1.0 / math.sqrt(qk_width)
    doc_ends = jnp.cumsum(doc_lengths)
    first_pos = lax.axis_index("ctx") * tokens
    q_pos = first_pos + jnp.arange(tokens, dtype=jnp.int32)
    q_doc = document(q_pos, doc_ends)
    q_rows = query.reshape(tokens, heads, qk_width)
    q_lat = jnp.einsum(
        "thn,hln->htl", q_rows[:, :, :NOPE], w_uk, preferred_element_type=jnp.float32
    ).astype(jnp.bfloat16)
    q_full = jnp.concatenate(
        [q_lat, jnp.transpose(q_rows[:, :, NOPE:], (1, 0, 2))], axis=2
    ).reshape(heads * tokens, LAT + ROPE)
    row_pos = jnp.tile(q_pos, heads)
    row_doc = jnp.tile(q_doc, heads)
    row_count = heads * tokens
    local_experts = w_in.shape[0]
    experts = local_experts * count_ctx
    own_gates = three_terms(dense_gates(routes, gate_weights, experts))
    width = LAT + ROPE
    spare = -(width + 3 * experts) % 128
    packed = jnp.concatenate(
        [latent, *own_gates, jnp.zeros((tokens, spare), jnp.bfloat16)], axis=1
    )
    packed = gather(count_ctx, 1, packed, None, None, 0)
    piece = packed[:, :width]
    all_gates = jnp.sum(
        packed[:, width : width + 3 * experts].astype(jnp.float32).reshape(-1, 3, experts), axis=1
    )
    first_expert = lax.axis_index("ctx") * local_experts
    gates = lax.dynamic_slice_in_dim(all_gates, first_expert, local_experts, axis=1)
    key_pos = jnp.arange(piece.shape[0], dtype=jnp.int32)
    key_doc = document(key_pos, doc_ends)
    allowed = (row_doc[:, None] == key_doc[None, :]) & (row_pos[:, None] >= key_pos[None, :])
    row_max = jnp.full((row_count,), -1e30, jnp.float32)
    scores = jnp.dot(q_full, piece.T, preferred_element_type=jnp.float32) * score_scale
    scores = jnp.where(allowed, scores, -1e30)
    new_max = jnp.maximum(row_max, jnp.max(scores, axis=1))
    weights = jnp.where(allowed, jnp.exp(scores - new_max[:, None]), 0.0)
    row_total = jnp.sum(weights, axis=1)
    accumulated = jnp.dot(
        weights.astype(jnp.bfloat16), piece[:, :LAT], preferred_element_type=jnp.float32
    )
    row_max, row_total, accumulated = (new_max, row_total, accumulated)
    o_lat = (accumulated / row_total[:, None]).astype(jnp.bfloat16).reshape(heads, tokens, LAT)
    head_out = (
        jnp.einsum("htl,hlv->thv", o_lat, w_uv, preferred_element_type=jnp.float32)
        .astype(jnp.bfloat16)
        .reshape(tokens, heads * VDIM)
    )
    local_width = residual.shape[1]
    attn_t = lax.psum_scatter(
        lax.dot_general(
            w_o, head_out, (((0,), (1,)), ((), ())), preferred_element_type=jnp.float32
        ).astype(jnp.bfloat16),
        "exp",
        scatter_dimension=0,
        tiled=True,
    ).astype(jnp.float32)
    hidden = residual.astype(jnp.float32) + attn_t.T
    squares = jnp.sum(hidden * hidden, axis=1)
    scaled = (hidden * norm_gain[None, :]).astype(jnp.bfloat16)
    hidden_pre, squares = gather(
        count_ctx,
        count_exp,
        scaled,
        jnp.broadcast_to(squares[None, :], (8, tokens)),
        jnp.transpose(w_in, (1, 0, 2, 3)).reshape(w_in.shape[1], -1),
        1,
    )
    squares = jnp.sum(squares.reshape(count_ctx, count_exp, 8, tokens)[:, :, 0], axis=1)
    inverse = lax.rsqrt(squares.reshape(-1) / D + epsilon)
    activated = activate(hidden_pre, inverse, gates)
    mixed = scatter(count_ctx, count_exp, activated, w_out.reshape(-1, w_out.shape[2]), 2)
    return (hidden + mixed).astype(jnp.bfloat16)


def solution(mesh):
    placed = (
        P("ctx", None),
        P("ctx", "exp"),
        P("exp", None, None),
        P("exp", None, None),
        P("exp", None),
        P("ctx", "exp"),
        P("exp"),
        P("ctx", None, None, "exp"),
        P("ctx", "exp", None),
        P("ctx", None),
        P("ctx", None),
        P(),
    )
    return jax.shard_map(
        body, mesh=mesh, in_specs=placed, out_specs=P("ctx", "exp"), check_vma=False
    )
```

```python
import functools
import math

import jax
import jax.numpy as jnp
from jax import lax
from jax.experimental import pallas as pl
from jax.experimental.pallas import tpu as pltpu
from jax.sharding import PartitionSpec as P

D = 4096
NOPE = 128
ROPE = 64
LAT = 512
VDIM = 128
TOP = 8


epsilon = 1e-06


def document(positions, doc_ends):
    return jnp.sum((positions[:, None] >= doc_ends[None, :]).astype(jnp.int32), axis=1)


MESH = pl.DeviceIdType.MESH


def ring_place(chip, chips):
    half = chips // 2
    return chip + (chip // half) * (chips - 1 + half - 2 * chip)


def ring_member(place, chips, core):
    return ring_place(lax.rem(place + chips, chips), chips) * 2 + core


def by_distance(count):
    return sorted(range(count), key=lambda step: min(step, count - step))


def greet(peers):
    barrier = pltpu.get_barrier_semaphore()
    for peer in peers:
        pl.semaphore_signal(barrier, inc=1, device_id=peer, device_id_type=MESH)
    pl.semaphore_wait(barrier, len(peers))


def neighbours(chips, count_exp):
    ctx, exp = lax.axis_index("ctx"), lax.axis_index("exp")
    core = lax.rem(ctx, 2)
    place = ring_place(ctx // 2, chips)
    sibling = (ctx + 1 - 2 * core, exp)
    right = (ring_member(place + 1, chips, core), exp)
    left = (ring_member(place - 1, chips, core), exp)
    across = [(ctx, lax.rem(exp + step, count_exp)) for step in range(count_exp)]
    return ctx, exp, core, place, sibling, (right, left), across


def gather_kernel(chips, count_exp, with_extra, *refs):
    if with_extra:
        own_ref, extra_ref, weight_ref, product_ref, extra_out, out_ref, weight, weight_sem = refs[:8]
        refs = refs[8:]
    else:
        own_ref, out_ref = refs[:2]
        extra_ref = extra_out = None
        refs = refs[2:]
    local_sem, z_send, z_recv, ring_send, ring_recv, sib_send, sib_recv = refs
    ctx, exp, core, place, sibling, sides, across = neighbours(chips, count_exp)
    half = chips // 2
    rows, cols = own_ref.shape
    chunks = by_distance(count_exp) + (["extra"] if with_extra else [])
    slot_of = {chunk: at for at, chunk in enumerate(chunks)}
    greet([*across[1:], *sides, sibling])

    def block(owner, chunk, part):
        if chunk == "extra":
            height = extra_ref.shape[0] * count_exp
            return extra_out.at[pl.ds(pl.multiple_of(owner * height, height), height)]
        start, height = (0, rows) if part is None else (part * (rows // 2), rows // 2)
        down = pl.ds(pl.multiple_of(owner * rows + start, rows // 2), height)
        if count_exp == 1:
            return out_ref.at[down]
        column = lax.rem(exp - chunk + count_exp, count_exp) * cols
        return out_ref.at[down, pl.ds(pl.multiple_of(column, cols), cols)]

    def extra_block(which):
        height = extra_ref.shape[0]
        at = (ctx * count_exp + which) * height
        return extra_out.at[pl.ds(pl.multiple_of(at, height), height)]

    started = []

    def send(source, target, sems, at, device):
        copy = pltpu.make_async_remote_copy(
            src_ref=source,
            dst_ref=target,
            send_sem=sems[0].at[at],
            recv_sem=sems[1].at[at],
            device_id=device,
            device_id_type=MESH,
        )
        copy.start()
        started.append(copy)
        return copy

    loads = {}
    if with_extra:
        for chunk in by_distance(count_exp):
            first = lax.rem(exp - chunk + count_exp, count_exp) * cols
            halves, experts, _, units = weight_ref.shape
            loads[chunk] = [
                pltpu.make_async_copy(
                    weight_ref.at[at // experts, at % experts, pl.ds(pl.multiple_of(first, cols), cols)],
                    weight.at[chunk, :, pl.ds(at * units, units)],
                    weight_sem.at[chunk * halves * experts + at],
                )
                for at in range(halves * experts)
            ]

    def multiply(chunk):
        for load in loads[chunk]:
            load.wait()
        for copy in sib_of[chunk]:
            copy.wait_recv()
        first = lax.rem(exp - chunk + count_exp, count_exp) * cols
        chosen = pl.ds(pl.multiple_of(first, cols), cols)
        tall, wide = 512, 256
        across_tiles = product_ref.shape[1] // wide

        def tile(at, carry):
            down = pl.ds(pl.multiple_of(at // across_tiles * tall, tall), tall)
            side = pl.ds(pl.multiple_of(lax.rem(at, across_tiles) * wide, wide), wide)
            product = jnp.dot(
                out_ref[down, chosen], weight[chunk, :, side], preferred_element_type=jnp.float32
            )
            product_ref[down, side] = product if chunk == 0 else product_ref[down, side] + product
            return carry

        lax.fori_loop(0, product_ref.shape[0] // tall * across_tiles, tile, 0)

    keeps = [pltpu.make_async_copy(own_ref, block(ctx, 0, None), local_sem.at[0])]
    if with_extra:
        keeps.append(pltpu.make_async_copy(extra_ref, extra_block(exp), local_sem.at[1]))
    for keep in keeps:
        keep.start()
    arriving = {}
    z_sems = (z_send, z_recv)
    for step in range(1, count_exp):
        if with_extra:
            arriving["extra", step] = send(
                extra_ref, extra_block(exp), z_sems, count_exp + step, across[step]
            )
    for step in by_distance(count_exp)[1:]:
        arriving[step] = send(own_ref, block(ctx, 0, None), z_sems, step, across[step])
    for chunk in loads:
        for load in loads[chunk]:
            load.start()
    for keep in keeps:
        keep.wait()

    ring_sems, sib_sems = (ring_send, ring_recv), (sib_send, sib_recv)
    ring, sib_of = {}, {chunk: [] for chunk in chunks}

    def share(owner, chunk, part, at):
        piece = block(owner, chunk, part)
        sib_of[chunk].append(send(piece, piece, sib_sems, at, sibling))

    def hop_on(chunk, hop, side):
        if chunk == "extra" and hop == half and side == 1:
            return
        part = side if hop == half and chunk != "extra" else None
        source = ring_member(place - (hop - 1) * (1 - 2 * side), chips, core)
        piece = block(source, chunk, part)
        at = (side * half + hop - 1) * len(chunks) + slot_of[chunk]
        ring[chunk, hop, side] = send(piece, piece, ring_sems, at, sides[side])

    def arrive(chunk, hop):
        for side in range(2):
            if (chunk, hop, side) not in ring:
                continue
            ring[chunk, hop, side].wait_recv()
            if hop < half:
                hop_on(chunk, hop + 1, side)
        for side in range(2):
            if (chunk, hop, side) not in ring:
                continue
            part = side if hop == half and chunk != "extra" else None
            source = ring_member(place - hop * (1 - 2 * side), chips, core)
            at = len(chunks) + (side * half + hop - 1) * len(chunks) + slot_of[chunk]
            share(source, chunk, part, at)

    for turn in range(len(chunks) + half + 1):
        if turn < len(chunks):
            chunk = chunks[turn]
            if chunk == "extra":
                for step in range(1, count_exp):
                    arriving["extra", step].wait_recv()
            elif chunk != 0:
                arriving[chunk].wait_recv()
            for side in range(2):
                hop_on(chunk, 1, side)
            share(ctx, chunk, None, slot_of[chunk])
        for hop in range(1, half):
            if 0 <= turn - hop < len(chunks):
                arrive(chunks[turn - hop], hop)
        done = turn - half - 1
        if 0 <= done < len(chunks) and chunks[done] in loads:
            multiply(chunks[done])
        if 0 <= turn - half < len(chunks):
            arrive(chunks[turn - half], half)
    for chunk in chunks:
        if chunk not in loads:
            for copy in sib_of[chunk]:
                copy.wait_recv()
    for copy in started:
        copy.wait_send()


def gather(count_ctx, count_exp, own, extra, weight, collective_id):
    chips = count_ctx // 2
    half = chips // 2
    rows, cols = own.shape
    outs = [jax.ShapeDtypeStruct((count_ctx * rows, count_exp * cols), own.dtype)]
    operands = [own]
    place, space, held = pl.ANY, None, []
    dma = pltpu.SemaphoreType.DMA
    if extra is not None:
        operands += [extra, weight]
        wide = weight.shape[0] * weight.shape[1] * weight.shape[3]
        held = [
            pltpu.VMEM(outs[0].shape, own.dtype),
            pltpu.VMEM((count_exp, cols, wide), weight.dtype),
            dma((count_exp * weight.shape[0] * weight.shape[1],)),
        ]
        outs = [jax.ShapeDtypeStruct((count_ctx * rows, wide), jnp.float32)]
        place, space = pltpu.VMEM, 52 * 1024 * 1024
        outs.append(
            jax.ShapeDtypeStruct((count_ctx * count_exp * extra.shape[0], extra.shape[1]), extra.dtype)
        )
    chunks = count_exp + len(outs) - 1
    result = pl.pallas_call(
        functools.partial(gather_kernel, chips, count_exp, extra is not None),
        out_shape=outs,
        in_specs=[pl.BlockSpec(memory_space=pl.ANY)] * len(operands),
        out_specs=[pl.BlockSpec(memory_space=place)] + [pl.BlockSpec(memory_space=pl.ANY)] * (len(outs) - 1),
        scratch_shapes=[
            *held,
            dma((2,)),
            dma((2 * count_exp,)),
            dma((2 * count_exp,)),
            dma((2 * half * chunks,)),
            dma((2 * half * chunks,)),
            dma(((2 * half + 1) * chunks,)),
            dma(((2 * half + 1) * chunks,)),
        ],
        compiler_params=pltpu.CompilerParams(
            collective_id=collective_id, has_side_effects=True, vmem_limit_bytes=space
        ),
    )(*operands)
    return result if extra is not None else result[0]


def scatter_kernel(
    chips, count_exp, rows_ref, weight_ref, out_ref, weight, held, passed, landed, leaving, returned,
    load_sem, sib_send, sib_recv, ring_send, ring_recv, z_send, z_recv,
):
    ctx, exp, core, place, sibling, sides, across = neighbours(chips, count_exp)
    half = chips // 2
    rows, cols = out_ref.shape
    order = by_distance(count_exp)[::-1]
    greet([*across[1:], *sides, sibling])

    def block(owner, chunk):
        return held.at[chunk, pl.ds(pl.multiple_of(owner * rows, rows), rows)]

    started = []

    def send(source, target, sems, at, device):
        copy = pltpu.make_async_remote_copy(
            src_ref=source,
            dst_ref=target,
            send_sem=sems[0].at[at],
            recv_sem=sems[1].at[at],
            device_id=device,
            device_id_type=MESH,
        )
        copy.start()
        started.append(copy)
        return copy

    loads, swaps = {}, {}
    offsets = sorted(range(chips), key=lambda offset: -min(offset, chips - offset))
    for chunk in order:
        column = pl.ds(pl.multiple_of(across[chunk][1] * cols, cols), cols)
        loads[chunk] = pltpu.make_async_copy(
            weight_ref.at[:, column], weight.at[chunk], load_sem.at[chunk]
        )
        loads[chunk].start()

    def multiply(chunk):
        loads[chunk].wait()
        tall, wide = 512, 256
        across_tiles = cols // wide

        def tile(at, carry):
            down = pl.ds(pl.multiple_of(at // across_tiles * tall, tall), tall)
            side = pl.ds(pl.multiple_of(lax.rem(at, across_tiles) * wide, wide), wide)
            held[chunk, down, side] = jnp.dot(
                rows_ref[down], weight[chunk, :, side], preferred_element_type=jnp.float32
            ).astype(held.dtype)
            return carry

        lax.fori_loop(0, rows_ref.shape[0] // tall * across_tiles, tile, 0)
        for offset in offsets:
            at = offset * count_exp + chunk
            theirs = ring_member(place + offset, chips, 1 - core)
            swaps[offset, chunk] = send(
                block(theirs, chunk), passed.at[at], (sib_send, sib_recv), at, sibling
            )

    def mine(offset):
        return pl.multiple_of(ring_member(place + offset, chips, core) * rows, rows)

    def pair(offset, chunk):
        swaps[offset, chunk].wait_recv()
        at = offset * count_exp + chunk
        ours = held[chunk, pl.ds(mine(offset), rows)]
        return ours.astype(jnp.float32) + passed[at].astype(jnp.float32)

    ring = {}
    stretch = rows // 2

    def ring_slot(side, step, chunk):
        return (side * half + step - 1) * count_exp + chunk

    def pass_on(offset, side, step, chunk):
        slot = ring_slot(side, step, chunk)
        start, height = (side * stretch, stretch) if step == 1 else (0, rows)
        source = held.at[chunk, pl.ds(pl.multiple_of(mine(offset) + start, stretch), height)]
        target = landed.at[slot, pl.ds(start, height)]
        ring[side, step, chunk] = send(source, target, (ring_send, ring_recv), slot, sides[side])

    def begin(chunk):
        held[chunk, pl.ds(mine(half), rows)] = pair(half, chunk).astype(held.dtype)
        for side in range(2):
            pass_on(half, side, 1, chunk)

    def middle(chunk, step):
        for side in range(2):
            offset = half - step + 1
            offset = offset if side == 0 else chips - offset
            total = pair(offset, chunk)
            ring[side, step - 1, chunk].wait_recv()
            slot = ring_slot(side, step - 1, chunk)
            if step == 2:
                came = landed[slot, pl.ds(side * stretch, stretch)].astype(jnp.float32)
                parts = [total[:stretch], total[stretch:]]
                parts[side] = parts[side] + came
                for which in range(2):
                    down = pl.ds(pl.multiple_of(mine(offset) + which * stretch, stretch), stretch)
                    held[chunk, down] = parts[which].astype(held.dtype)
            else:
                total = total + landed[slot].astype(jnp.float32)
                held[chunk, pl.ds(mine(offset), rows)] = total.astype(held.dtype)
            pass_on(offset, side, step, chunk)

    back = {}

    def finish(chunk):
        total = pair(0, chunk)
        for side in range(2):
            ring[side, half, chunk].wait_recv()
            total += landed[ring_slot(side, half, chunk)].astype(jnp.float32)
        if chunk == 0:
            out_ref[...] = total
        else:
            leaving[chunk] = total.astype(leaving.dtype)
            back[chunk] = send(
                leaving.at[chunk], returned.at[chunk], (z_send, z_recv), chunk, across[chunk]
            )

    multiply(order[0])
    for turn in range(count_exp + half):
        if turn + 1 < count_exp:
            multiply(order[turn + 1])
        if turn < count_exp:
            begin(order[turn])
        for step in range(2, half + 1):
            if 0 <= turn - step + 1 < count_exp:
                middle(order[turn - step + 1], step)
        if 0 <= turn - half < count_exp:
            finish(order[turn - half])
    total = out_ref[...]
    for chunk in order[:-1]:
        back[chunk].wait_recv()
        total += returned[chunk].astype(jnp.float32)
    out_ref[...] = total
    for copy in started:
        copy.wait_send()


def scatter(count_ctx, count_exp, rows_in, weight, collective_id):
    chips = count_ctx // 2
    half = chips // 2
    rows, cols = rows_in.shape[0] // count_ctx, weight.shape[1] // count_exp
    dma = pltpu.SemaphoreType.DMA
    blocks, hops = chips * count_exp, 2 * half * count_exp
    kind = rows_in.dtype
    return pl.pallas_call(
        functools.partial(scatter_kernel, chips, count_exp),
        out_shape=jax.ShapeDtypeStruct((rows, cols), jnp.float32),
        in_specs=[pl.BlockSpec(memory_space=pltpu.VMEM), pl.BlockSpec(memory_space=pl.ANY)],
        out_specs=pl.BlockSpec(memory_space=pltpu.VMEM),
        scratch_shapes=[
            pltpu.VMEM((count_exp, weight.shape[0], cols), kind),
            pltpu.VMEM((count_exp, rows_in.shape[0], cols), kind),
            pltpu.VMEM((blocks, rows, cols), kind),
            pltpu.VMEM((hops, rows, cols), kind),
            pltpu.VMEM((count_exp, rows, cols), kind),
            pltpu.VMEM((count_exp, rows, cols), kind),
            dma((count_exp,)),
            dma((blocks,)),
            dma((blocks,)),
            dma((hops,)),
            dma((hops,)),
            dma((count_exp,)),
            dma((count_exp,)),
        ],
        compiler_params=pltpu.CompilerParams(
            collective_id=collective_id, has_side_effects=True, vmem_limit_bytes=52 * 1024 * 1024
        ),
    )(rows_in, weight)


def three_terms(values):
    first = lax.reduce_precision(values, 8, 7)
    second = lax.reduce_precision(values - first, 8, 7)
    third = values - first - second
    return [term.astype(jnp.bfloat16) for term in (first, second, third)]


def dense_gates(routes, gate_weights, experts):
    hit = routes[:, :, None] == jnp.arange(experts, dtype=jnp.int32)[None, None, :]
    return jnp.sum(jnp.where(hit, gate_weights[:, :, None], 0.0), axis=1)


def activate(hidden_pre, inverse, gates):
    width = hidden_pre.shape[1] // 2
    experts = gates.shape[1]
    owner = lax.broadcasted_iota(jnp.int32, (1, width), 1) // (width // experts)
    wide_gates = jnp.zeros((1, width), jnp.float32)
    for expert in range(experts):
        wide_gates = jnp.where(owner == expert, gates[:, expert][:, None], wide_gates)
    gate, up = hidden_pre[:, :width] * inverse[:, None], hidden_pre[:, width:] * inverse[:, None]
    return (jax.nn.silu(gate) * up * wide_gates).astype(jnp.bfloat16)


def body(
    latent,
    query,
    w_uk,
    w_uv,
    w_o,
    residual,
    norm_gain,
    w_in,
    w_out,
    routes,
    gate_weights,
    doc_lengths,
):
    count_ctx, count_exp = lax.axis_size("ctx"), lax.axis_size("exp")
    tokens = latent.shape[0]
    heads = w_uk.shape[0]
    qk_width = NOPE + ROPE
    score_scale = 1.0 / math.sqrt(qk_width)
    doc_ends = jnp.cumsum(doc_lengths)
    first_pos = lax.axis_index("ctx") * tokens
    q_pos = first_pos + jnp.arange(tokens, dtype=jnp.int32)
    q_doc = document(q_pos, doc_ends)
    q_rows = query.reshape(tokens, heads, qk_width)
    q_lat = jnp.einsum(
        "thn,hln->htl", q_rows[:, :, :NOPE], w_uk, preferred_element_type=jnp.float32
    ).astype(jnp.bfloat16)
    q_full = jnp.concatenate(
        [q_lat, jnp.transpose(q_rows[:, :, NOPE:], (1, 0, 2))], axis=2
    ).reshape(heads * tokens, LAT + ROPE)
    row_pos = jnp.tile(q_pos, heads)
    row_doc = jnp.tile(q_doc, heads)
    row_count = heads * tokens
    local_experts = w_in.shape[0]
    experts = local_experts * count_ctx
    own_gates = three_terms(dense_gates(routes, gate_weights, experts))
    width = LAT + ROPE
    spare = -(width + 3 * experts) % 128
    packed = jnp.concatenate(
        [latent, *own_gates, jnp.zeros((tokens, spare), jnp.bfloat16)], axis=1
    )
    packed = gather(count_ctx, 1, packed, None, None, 0)
    piece = packed[:, :width]
    all_gates = jnp.sum(
        packed[:, width : width + 3 * experts].astype(jnp.float32).reshape(-1, 3, experts), axis=1
    )
    first_expert = lax.axis_index("ctx") * local_experts
    gates = lax.dynamic_slice_in_dim(all_gates, first_expert, local_experts, axis=1)
    key_pos = jnp.arange(piece.shape[0], dtype=jnp.int32)
    key_doc = document(key_pos, doc_ends)
    allowed = (row_doc[:, None] == key_doc[None, :]) & (row_pos[:, None] >= key_pos[None, :])
    row_max = jnp.full((row_count,), -1e30, jnp.float32)
    scores = jnp.dot(q_full, piece.T, preferred_element_type=jnp.float32) * score_scale
    scores = jnp.where(allowed, scores, -1e30)
    new_max = jnp.maximum(row_max, jnp.max(scores, axis=1))
    weights = jnp.where(allowed, jnp.exp(scores - new_max[:, None]), 0.0)
    row_total = jnp.sum(weights, axis=1)
    accumulated = jnp.dot(
        weights.astype(jnp.bfloat16), piece[:, :LAT], preferred_element_type=jnp.float32
    )
    row_max, row_total, accumulated = (new_max, row_total, accumulated)
    o_lat = (accumulated / row_total[:, None]).astype(jnp.bfloat16).reshape(heads, tokens, LAT)
    head_out = (
        jnp.einsum("htl,hlv->thv", o_lat, w_uv, preferred_element_type=jnp.float32)
        .astype(jnp.bfloat16)
        .reshape(tokens, heads * VDIM)
    )
    local_width = residual.shape[1]
    attn_t = lax.psum_scatter(
        lax.dot_general(
            w_o, head_out, (((0,), (1,)), ((), ())), preferred_element_type=jnp.float32
        ).astype(jnp.bfloat16),
        "exp",
        scatter_dimension=0,
        tiled=True,
    ).astype(jnp.float32)
    hidden = residual.astype(jnp.float32) + attn_t.T
    squares = jnp.sum(hidden * hidden, axis=1)
    scaled = (hidden * norm_gain[None, :]).astype(jnp.bfloat16)
    hidden_pre, squares = gather(
        count_ctx,
        count_exp,
        scaled,
        jnp.broadcast_to(squares[None, :], (8, tokens)),
        jnp.transpose(w_in, (2, 0, 1, 3)),
        1,
    )
    squares = jnp.sum(squares.reshape(count_ctx, count_exp, 8, tokens)[:, :, 0], axis=1)
    inverse = lax.rsqrt(squares.reshape(-1) / D + epsilon)
    activated = activate(hidden_pre, inverse, gates)
    mixed = scatter(count_ctx, count_exp, activated, w_out.reshape(-1, w_out.shape[2]), 2)
    return (hidden + mixed).astype(jnp.bfloat16)


def solution(mesh):
    placed = (
        P("ctx", None),
        P("ctx", "exp"),
        P("exp", None, None),
        P("exp", None, None),
        P("exp", None),
        P("ctx", "exp"),
        P("exp"),
        P("ctx", None, None, "exp"),
        P("ctx", "exp", None),
        P("ctx", None),
        P("ctx", None),
        P(),
    )
    return jax.shard_map(
        body, mesh=mesh, in_specs=placed, out_specs=P("ctx", "exp"), check_vma=False
    )
```
